32 devices in a mesh: view: 4 (over y, x), row: 4 (over z), disp: 2 (over core).
Axes of the slice: x: 2, y: 2, z: 4, core: 2. Of those that a mesh axis runs over, the one named last changes fastest.
Arguments:
- images: float32 [4, 32, 2048], P('view', 'row')
- sharpness: float32 [4], P('view'), may hold values from 1 to 800
- paired: int32 [4, 2], P('view'), may hold values from 0 to 1, as said below
- offset: int32 [4, 2], P('view'), may hold values from 0 to 127
- row_range: int32 [4, 2, 2], P('view'), may hold values from 0 to 32, as said below
Outputs:
- left_disparity: float32 [4, 2, 32, 2048], P('view', None, 'row')
- right_disparity: float32 [4, 2, 32, 2048], P('view', None, 'row')
The draws below stay inside these ranges and needn't reach their ends.
Inputs may be any that keep to these rules, and one draw needn't show every extreme that they name: paired[v, j] is 0 whenever v + j + 1 >= 4. row_range[v, j, 0] <= 8 and row_range[v, j, 1] >= 24.
All inputs are finite; a program needn't handle non-finite values.
Results may differ from the reference program's by a relative error of at most 0.0003.
Values sent between devices are 32-bit elements; how exact they have to be, the bound alone decides.
A program may use at most 192 MiB of HBM per device.

```python
import math
import jax
import jax.numpy as jnp
from jax import lax

DISP = 256
RAD = 4
SLOTS = 2
OFFMAX = 128
COLS = 2048
VIEWS = 4
ROWS = 32


def draw_images(key, part):
    first_key, second_key, third_key = jax.random.split(key, 3)
    noise = jax.random.normal(first_key, (VIEWS, ROWS, COLS), jnp.float32)
    row_gain = jax.random.uniform(second_key, (VIEWS, ROWS, 1), jnp.float32, 0.0, 1.15)
    col_gain = jax.random.uniform(third_key, (VIEWS, 1, COLS), jnp.float32, 0.0, 1.15)
    contrast = jnp.exp(row_gain + col_gain)
    return noise * contrast


def draw_paired(key, part):
    coin_flips = jax.random.randint(key, (VIEWS, SLOTS), 0, 4)
    view_index = jnp.arange(VIEWS, dtype=jnp.int32)
    in_block = view_index[:, None] + jnp.arange(SLOTS, dtype=jnp.int32)[None, :] + 1 < VIEWS
    chosen = jax.random.randint(jax.random.fold_in(key, 1), (), 0, VIEWS - SLOTS)
    forced = view_index[:, None] == chosen
    active = ((coin_flips > 0) | forced) & in_block
    return active.astype(jnp.int32)


def draw_offset(key, part):
    shifts = jax.random.randint(key, (VIEWS * SLOTS,), 0, OFFMAX)
    ordering = jax.random.permutation(jax.random.fold_in(key, 2), VIEWS * SLOTS)
    shifts = shifts.at[ordering[0]].set(OFFMAX - 1).at[ordering[1]].set(0)
    return shifts.reshape(VIEWS, SLOTS)


def draw_row_range(key, part):
    quarter = ROWS // 4
    lower_row = jax.random.randint(key, (VIEWS * SLOTS,), 0, quarter + 1)
    upper_row = ROWS - jax.random.randint(jax.random.fold_in(key, 3), (VIEWS * SLOTS,), 0, quarter + 1)
    ordering = jax.random.permutation(jax.random.fold_in(key, 4), VIEWS * SLOTS)
    lower_row = lower_row.at[ordering[0]].set(0).reshape(VIEWS, SLOTS)
    upper_row = upper_row.at[ordering[1]].set(ROWS).reshape(VIEWS, SLOTS)
    return jnp.stack([lower_row, upper_row], axis=-1)


def level_of(rng, extent, cuts, low, high):
    level, own = 1.0, jax.random.fold_in(rng, 6)
    for position, blocks in cuts:
        heights = jnp.exp(jax.random.uniform(jax.random.fold_in(own, position), (blocks,), jnp.float32, low / len(cuts), high / len(cuts)))
        level = level * jnp.repeat(heights, extent[position] // blocks).reshape([-1 if axis == position else 1 for axis in range(len(extent))])
    return level


def setup_inputs(seed: int = 0) -> dict:
    streams_of = jax.random.split(jax.random.key(seed), 6)
    return {
        "images": draw_images(jax.random.fold_in(streams_of[5], 71), 0),
        "sharpness": jnp.clip(jnp.exp(math.log(800.0) - 6.684612 * jax.random.uniform(streams_of[1], (VIEWS,), jnp.float32) ** level_of(streams_of[1], (VIEWS,), ((0, 4),), -0.2, 0.2)), 1.0, 800.0),
        "paired": draw_paired(jax.random.fold_in(streams_of[5], 71), 0),
        "offset": draw_offset(jax.random.fold_in(streams_of[5], 71), 0),
        "row_range": draw_row_range(jax.random.fold_in(streams_of[5], 71), 0),
    }


EPSILON = 1e-05

def box_sum(field):
    row_count = field.shape[-2] - 2 * RAD
    col_count = field.shape[-1]
    running = field[..., 0:row_count, :]
    for offset_row in range(1, 2 * RAD + 1):
        running = running + field[..., offset_row:offset_row + row_count, :]
    widths = [(0, 0)] * (running.ndim - 1) + [(RAD, RAD)]
    padded = jnp.pad(running, widths)
    summed = padded[..., 0:col_count]
    for offset_col in range(1, 2 * RAD + 1):
        summed = summed + padded[..., offset_col:offset_col + col_count]
    return summed

def window_stats(rimmed):
    window = float((2 * RAD + 1) ** 2)
    center = box_sum(rimmed) / window
    spread = box_sum(rimmed * rimmed) / window - center * center
    return (center, spread)

def pair_disparity(left_image, right_image, shift_base, sharp_value):
    pad_cols = DISP + OFFMAX
    left_rim = jnp.pad(left_image, ((RAD, RAD), (0, 0)))
    right_rim = jnp.pad(right_image, ((RAD, RAD), (0, 0)))
    left_mean, left_var = window_stats(left_rim)
    right_mean, right_var = window_stats(right_rim)
    right_wide = jnp.pad(right_rim, ((0, 0), (pad_cols, 0)))
    mean_wide = jnp.pad(right_mean, ((0, 0), (pad_cols, 0)))
    var_wide = jnp.pad(right_var, ((0, 0), (pad_cols, 0)))
    column = jnp.arange(COLS, dtype=jnp.int32)
    window = float((2 * RAD + 1) ** 2)
    zero_index = jnp.zeros((), jnp.int32)

    def one_disparity(level):
        amount = (level + shift_base).astype(jnp.int32)
        start_col = (pad_cols - amount).astype(jnp.int32)
        moved_strip = lax.dynamic_slice(right_wide, (zero_index, start_col), (ROWS + 2 * RAD, COLS))
        cross_sum = box_sum(left_rim * moved_strip) / window
        moved_mean = lax.dynamic_slice(mean_wide, (zero_index, start_col), (ROWS, COLS))
        moved_var = lax.dynamic_slice(var_wide, (zero_index, start_col), (ROWS, COLS))
        ncc_left = (cross_sum - left_mean * moved_mean) * lax.rsqrt((left_var + EPSILON) * (moved_var + EPSILON))
        ncc_left = jnp.where(column[None, :] >= amount, ncc_left, -1.0)
        extended = jnp.pad(ncc_left, ((0, 0), (0, pad_cols)), constant_values=-1.0)
        ncc_right = lax.dynamic_slice(extended, (zero_index, amount), (ROWS, COLS))
        return (ncc_left, ncc_right)
    levels = jnp.arange(DISP, dtype=jnp.int32)
    ncc_left, ncc_right = lax.map(one_disparity, levels)
    values = levels.astype(ncc_left.dtype) / DISP
    results = []
    for volume in (ncc_left, ncc_right):
        weights = jax.nn.softmax(sharp_value * volume, axis=0)
        results.append(lax.optimization_barrier(jnp.sum(weights * values[:, None, None], axis=0)))
    return (results[0], results[1])

def reference(images, sharpness, paired, offset, row_range):
    row_index = jnp.arange(ROWS, dtype=jnp.int32)
    left_list = []
    right_list = []
    for slot_index in range(SLOTS):

        def per_view(view_index):
            partner = jnp.minimum(view_index + slot_index + 1, VIEWS - 1)
            return pair_disparity(images[view_index], images[partner], offset[view_index, slot_index], sharpness[view_index])
        left_slot, right_slot = lax.map(per_view, jnp.arange(VIEWS, dtype=jnp.int32))
        inside = (row_index[None, :] >= row_range[:, slot_index, 0:1]) & (row_index[None, :] < row_range[:, slot_index, 1:2])
        keeping = paired[:, slot_index].astype(left_slot.dtype)[:, None, None] * inside.astype(left_slot.dtype)[:, :, None]
        left_slot = left_slot * keeping
        right_slot = right_slot * keeping
        right_slot = jnp.concatenate([jnp.zeros((slot_index + 1, ROWS, COLS), left_slot.dtype), right_slot[:VIEWS - slot_index - 1]], axis=0)
        left_list.append(left_slot)
        right_list.append(right_slot)
    return (jnp.stack(left_list, axis=1), jnp.stack(right_list, axis=1))
```

```python
import functools
import math

import jax
import jax.numpy as jnp
from jax import lax
from jax.experimental import pallas as pl
from jax.experimental.pallas import tpu as pltpu
from jax.sharding import PartitionSpec as P

DISP = 256
RAD = 4
TAPS = 2 * RAD + 1
EPSILON = 1e-05
DEPTH = 256
PAD = 128
FAR = -1e30


def rounded(value):
    return value.astype(jnp.bfloat16).astype(jnp.float32)


def split3(value):
    high = rounded(value)
    middle = rounded(value - high)
    return (high, middle, value - high - middle)


def build_patches(pad_ref, stat_ref, tail_ref, patch_ref, gain, valid, extras, order):
    cols = patch_ref.shape[1]
    top = pad_ref[0:8, :]
    last = pad_ref[8:9, :]
    stat_ref[0:1, :] = jnp.sum(top, axis=0, keepdims=True) + last
    stat_ref[1:2, :] = jnp.sum(top * top, axis=0, keepdims=True) + last * last
    total = stat_ref[0:2, PAD - RAD : PAD - RAD + cols]
    for tap in range(1, TAPS):
        begin = PAD - RAD + tap
        total = total + stat_ref[0:2, begin : begin + cols]
    total = total * (1.0 / (TAPS * TAPS))
    mean = total[0:1]
    var = total[1:2] - mean * mean
    scale = lax.rsqrt(var + EPSILON) * (gain * (1.0 / TAPS))
    if valid is not None:
        scale = jnp.where(valid, scale, 0.0)
    for tap in range(TAPS):
        begin = PAD - RAD + tap
        tail_ref[tap : tap + 1, :] = pad_ref[8:9, begin : begin + cols]
        value = (pad_ref[0:8, begin : begin + cols] - mean) * scale
        high = rounded(value)
        parts = (high, value - high)
        for group in range(3):
            start = group * 8 * TAPS + tap * 8
            patch_ref[start : start + 8, :] = parts[order[group]]
    value = (tail_ref[0:TAPS, :] - mean) * scale
    high = rounded(value)
    parts = (high, value - high)
    for group in range(3):
        start = 24 * TAPS + group * TAPS
        patch_ref[start : start + TAPS, :] = parts[order[group]]
    base = 27 * TAPS
    patch_ref[base:DEPTH, :] = jnp.zeros((DEPTH - base, cols), jnp.float32)
    for place, row in extras:
        patch_ref[base + place : base + place + 1, :] = row


def soft_side(rows_ref, cols_ref, score_ref, result_ref, left):
    count = result_ref.shape[1] // 256
    lane = lax.broadcasted_iota(jnp.int32, (8, 128), 1)
    sub = lax.broadcasted_iota(jnp.int32, (8, 128), 0)
    skew = lane - sub
    sub_f = sub.astype(jnp.float32)
    lane_f = lane[0:1].astype(jnp.float32)
    slack = 0 if left else 1
    steps = (DISP + 128) // 8

    def body(block, carry):
        start = pl.multiple_of(block * 256, 256)
        score_ref[...] = jnp.dot(
            rows_ref[pl.ds(start, 512), :],
            cols_ref[:, pl.ds(start, 256)],
            preferred_element_type=jnp.float32,
        )
        for half in range(2):

            def load(step):
                score = score_ref[half * 128 + step * 8 : half * 128 + step * 8 + 8, half * 128 : half * 128 + 128]
                if step < 16:
                    score = jnp.where(skew < 8 * step + slack, score, FAR)
                elif step >= steps - 16:
                    score = jnp.where(skew >= 8 * step - DISP + slack, score, FAR)
                return score

            tops = [load(0), load(1), load(2), load(3)]
            for step in range(4, steps):
                tops[step % 4] = jnp.maximum(tops[step % 4], load(step))
            top = jnp.maximum(jnp.maximum(tops[0], tops[1]), jnp.maximum(tops[2], tops[3]))
            top = jnp.broadcast_to(jnp.max(top, axis=0, keepdims=True), (8, 128))
            summed = jnp.zeros((8, 128), jnp.float32)
            running = jnp.zeros((8, 128), jnp.float32)
            for step in range(steps):
                summed = summed + jnp.exp2(load(step) - top)
                running = running + summed
            moment = 8.0 * (steps * summed - running) + sub_f * summed
            total = jnp.sum(summed, axis=0, keepdims=True)
            moment = jnp.sum(moment, axis=0, keepdims=True)
            if left:
                weighted = (lane_f + DISP) * total - moment
            else:
                weighted = moment - lane_f * total
            column = pl.multiple_of(start + half * 128, 128)
            result_ref[:, pl.ds(column, 128)] = weighted / (total * DISP)
        return carry

    lax.fori_loop(0, count, body, 0)


def match_kernel(
    views, slots, sharp_ref, meta_ref, bands_ref, out_ref,
    pad_ref, roll_ref, stat_ref, tail_ref, patch_ref,
    left_cols, left_rows, right_cols, right_rows, score_ref, result_ref,
):
    cols = patch_ref.shape[1]
    out_ref[...] = jnp.zeros_like(out_ref)
    pad_ref[...] = jnp.zeros_like(pad_ref)
    column = lax.broadcasted_iota(jnp.int32, (1, cols), 1)
    depth_at = lax.broadcasted_iota(jnp.int32, (1, DEPTH), 1) - 27 * TAPS
    ones = jnp.ones((1, cols), jnp.float32)
    flag = jnp.where((depth_at >= 0) & (depth_at < 6), 1.0, 0.0)
    for view in range(views):
        pad_ref[view, :, PAD : PAD + cols] = bands_ref[view]
    for view in range(1, views):
        build_patches(
            pad_ref.at[view], stat_ref, tail_ref, patch_ref, 1.0, None,
            [(3, ones), (4, ones), (5, ones)], (0, 1, 0),
        )
        whole = patch_ref[...].astype(jnp.bfloat16)
        right_cols[view - 1] = whole
        right_rows[view - 1, 0:DISP, :] = jnp.broadcast_to(flag, (DISP, DEPTH)).astype(jnp.bfloat16)
        right_rows[view - 1, DISP : DISP + cols, :] = whole.T
    for view in range(views - 1):
        for slot in range(min(slots, views - 1 - view)):
            partner = view + slot + 1
            index = view * slots + slot

            @pl.when(meta_ref[2, index] != 0)
            def _():
                shift = meta_ref[0, index]
                keep = jnp.broadcast_to(meta_ref[1, index].astype(jnp.float32), (1, cols))
                gain = sharp_ref[view] * math.log2(math.e)
                roll_ref[...] = pltpu.roll(pad_ref[view], cols + 2 * PAD - shift, 1)
                valid = column < cols - shift
                floor = [-part for part in split3(jnp.full((1, cols), gain, jnp.float32))]
                extras = [(place, floor[place]) for place in range(3)]
                extras += [(place + 3, jnp.where(valid, 0.0, floor[place])) for place in range(3)]
                build_patches(
                    roll_ref, stat_ref, tail_ref, patch_ref, gain, valid, extras, (0, 0, 1)
                )
                whole = patch_ref[...].astype(jnp.bfloat16)
                left_cols[...] = whole
                left_rows[0:cols, :] = whole.T
                splits = [-part for part in split3(jnp.full((1, DEPTH), gain, jnp.float32))]
                ends = jnp.zeros((1, DEPTH), jnp.float32)
                for place in range(6):
                    ends = jnp.where(depth_at == place, splits[place % 3], ends)
                left_rows[cols : cols + DISP, :] = jnp.broadcast_to(ends, (DISP, DEPTH)).astype(jnp.bfloat16)
                soft_side(right_rows.at[partner - 1], left_cols, score_ref, result_ref, True)
                moved = pltpu.roll(jnp.broadcast_to(result_ref[...], (8, cols)), shift, 1)[0:1]
                even = (DISP - 1) / (2.0 * DISP)
                place = view * 2 * slots + slot
                out_ref[place : place + 1, :] = jnp.where(column < shift, even, moved) * keep
                soft_side(left_rows, right_cols.at[partner - 1], score_ref, result_ref, False)
                place = partner * 2 * slots + slots + slot
                out_ref[place : place + 1, :] = result_ref[...] * keep


def match(sharp, meta, bands, slots):
    views, rows, cols = bands.shape
    smem = pl.BlockSpec(memory_space=pltpu.SMEM)
    vmem = pl.BlockSpec(memory_space=pltpu.VMEM)
    wide = cols + 2 * PAD
    return pl.pallas_call(
        functools.partial(match_kernel, views, slots),
        out_shape=jax.ShapeDtypeStruct((views * 2 * slots, cols), jnp.float32),
        in_specs=[smem, smem, vmem],
        out_specs=vmem,
        scratch_shapes=[
            pltpu.VMEM((views, rows, wide), jnp.float32),
            pltpu.VMEM((rows, wide), jnp.float32),
            pltpu.VMEM((8, wide), jnp.float32),
            pltpu.VMEM((16, cols), jnp.float32),
            pltpu.VMEM((DEPTH, cols), jnp.float32),
            pltpu.VMEM((DEPTH, cols), jnp.bfloat16),
            pltpu.VMEM((cols + DISP, DEPTH), jnp.bfloat16),
            pltpu.VMEM((views - 1, DEPTH, cols), jnp.bfloat16),
            pltpu.VMEM((views - 1, cols + DISP, DEPTH), jnp.bfloat16),
            pltpu.VMEM((512, 256), jnp.float32),
            pltpu.VMEM((1, cols), jnp.float32),
        ],
        compiler_params=pltpu.CompilerParams(vmem_limit_bytes=40 * 1024 * 1024),
    )(sharp, meta, bands)


def gather_inputs(image, packed):
    forward = [(i, i + 1) for i in range(lax.axis_size("row") - 1)]
    backward = [(target, source) for source, target in forward]
    low = lax.ppermute(image[-RAD:], "row", forward)
    high = lax.ppermute(image[:RAD], "row", backward)
    line = jnp.pad(packed[None], ((0, 7), (0, image.shape[1] - packed.shape[0])))
    stack = lax.all_gather(jnp.concatenate([low, image, high, line], axis=0), "view")
    rows = image.shape[0] + 2 * RAD
    return (stack[:, :rows], stack[:, rows, : packed.shape[0]])


def scatter_outputs(found, slots, row_count):
    views, disp = (lax.axis_size("view"), lax.axis_size("disp"))
    cols = found.shape[1]
    send = jnp.repeat(found.reshape(views, 2 * slots, cols), disp, axis=0)
    got = lax.all_to_all(send, ("view", "disp"), 0, 0, tiled=True)
    got = got.reshape(views * disp, 2 * slots, cols)[:: views * disp // row_count]
    got = jnp.swapaxes(got, 0, 1)
    return (got[:slots], got[slots:])


def shards(images, sharpness, paired, offset, row_range):
    image = images[0]
    row_count, cols = image.shape
    slots = paired.shape[1]
    views, disp = (lax.axis_size("view"), lax.axis_size("disp"))
    member = lax.axis_index("view") * disp + lax.axis_index("disp")
    local_row = member * row_count // (views * disp)
    ints = jnp.concatenate([paired[0], offset[0], row_range[0].reshape(-1)])
    packed = jnp.concatenate([sharpness, ints.astype(jnp.float32)])
    stack, packs = gather_inputs(image, packed)
    bands = lax.dynamic_slice_in_dim(stack, local_row, 2 * RAD + 1, axis=1)
    bands = jnp.pad(bands, ((0, 0), (0, 16 - 2 * RAD - 1), (0, 0)))
    sharp = packs[:, 0]
    ints = packs[:, 1:].astype(jnp.int32)
    pairing = ints[:, :slots]
    shift = ints[:, slots : 2 * slots]
    limits = ints[:, 2 * slots :].reshape(views, slots, 2)
    row = lax.axis_index("row") * row_count + local_row
    inside = (row >= limits[..., 0]) & (row < limits[..., 1])
    active = jnp.where(inside, pairing, 0)
    meta = jnp.stack([shift.reshape(-1), active.reshape(-1), active.reshape(-1)])
    found = match(sharp, meta, bands, slots)
    left, right = scatter_outputs(found, slots, row_count)
    return (left[None], right[None])


def solution(mesh):
    return jax.shard_map(
        shards,
        mesh=mesh,
        in_specs=(
            P("view", "row", None),
            P("view"),
            P("view", None),
            P("view", None),
            P("view", None, None),
        ),
        out_specs=(P("view", None, "row", None), P("view", None, "row", None)),
        check_vma=False,
    )
```

```python
import functools
import math

import jax
import jax.numpy as jnp
from jax import lax
from jax.experimental import pallas as pl
from jax.experimental.pallas import tpu as pltpu
from jax.sharding import PartitionSpec as P

DISP = 256
RAD = 4
TAPS = 2 * RAD + 1
EPSILON = 1e-05
DEPTH = 256
PAD = 128
FAR = -1e30


def rounded(value):
    return value.astype(jnp.bfloat16).astype(jnp.float32)


def split3(value):
    high = rounded(value)
    middle = rounded(value - high)
    return (high, middle, value - high - middle)


def build_patches(pad_ref, stat_ref, tail_ref, patch_ref, gain, valid, extras, order):
    cols = patch_ref.shape[1]
    top = pad_ref[0:8, :]
    last = pad_ref[8:9, :]
    stat_ref[0:1, :] = jnp.sum(top, axis=0, keepdims=True) + last
    stat_ref[1:2, :] = jnp.sum(top * top, axis=0, keepdims=True) + last * last
    total = stat_ref[0:2, PAD - RAD : PAD - RAD + cols]
    for tap in range(1, TAPS):
        begin = PAD - RAD + tap
        total = total + stat_ref[0:2, begin : begin + cols]
    total = total * (1.0 / (TAPS * TAPS))
    mean = total[0:1]
    var = total[1:2] - mean * mean
    scale = lax.rsqrt(var + EPSILON) * (gain * (1.0 / TAPS))
    if valid is not None:
        scale = jnp.where(valid, scale, 0.0)
    for tap in range(TAPS):
        begin = PAD - RAD + tap
        tail_ref[tap : tap + 1, :] = pad_ref[8:9, begin : begin + cols]
        value = (pad_ref[0:8, begin : begin + cols] - mean) * scale
        high = rounded(value)
        parts = (high, value - high)
        for group in range(3):
            start = group * 8 * TAPS + tap * 8
            patch_ref[start : start + 8, :] = parts[order[group]]
    value = (tail_ref[0:TAPS, :] - mean) * scale
    high = rounded(value)
    parts = (high, value - high)
    for group in range(3):
        start = 24 * TAPS + group * TAPS
        patch_ref[start : start + TAPS, :] = parts[order[group]]
    base = 27 * TAPS
    patch_ref[base:DEPTH, :] = jnp.zeros((DEPTH - base, cols), jnp.float32)
    for place, row in extras:
        patch_ref[base + place : base + place + 1, :] = row


def soft_side(rows_ref, cols_ref, score_ref, result_ref, left):
    count = result_ref.shape[1] // 256
    lane = lax.broadcasted_iota(jnp.int32, (8, 128), 1)
    sub = lax.broadcasted_iota(jnp.int32, (8, 128), 0)
    skew = lane - sub
    sub_f = sub.astype(jnp.float32)
    lane_f = lane[0:1].astype(jnp.float32)
    slack = 0 if left else 1
    steps = (DISP + 128) // 8

    def body(block, carry):
        start = pl.multiple_of(block * 256, 256)
        score_ref[...] = jnp.dot(
            rows_ref[pl.ds(start, 512), :],
            cols_ref[:, pl.ds(start, 256)],
            preferred_element_type=jnp.float32,
        )
        for half in range(2):

            def load(step):
                score = score_ref[half * 128 + step * 8 : half * 128 + step * 8 + 8, half * 128 : half * 128 + 128]
                if step < 16:
                    score = jnp.where(skew < 8 * step + slack, score, FAR)
                elif step >= steps - 16:
                    score = jnp.where(skew >= 8 * step - DISP + slack, score, FAR)
                return score

            tops = [load(0), load(1), load(2), load(3)]
            for step in range(4, steps):
                tops[step % 4] = jnp.maximum(tops[step % 4], load(step))
            top = jnp.maximum(jnp.maximum(tops[0], tops[1]), jnp.maximum(tops[2], tops[3]))
            top = jnp.broadcast_to(jnp.max(top, axis=0, keepdims=True), (8, 128))
            summed = jnp.zeros((8, 128), jnp.float32)
            running = jnp.zeros((8, 128), jnp.float32)
            for step in range(steps):
                summed = summed + jnp.exp2(load(step) - top)
                running = running + summed
            moment = 8.0 * (steps * summed - running) + sub_f * summed
            total = jnp.sum(summed, axis=0, keepdims=True)
            moment = jnp.sum(moment, axis=0, keepdims=True)
            if left:
                weighted = (lane_f + DISP) * total - moment
            else:
                weighted = moment - lane_f * total
            column = pl.multiple_of(start + half * 128, 128)
            result_ref[:, pl.ds(column, 128)] = weighted / (total * DISP)
        return carry

    lax.fori_loop(0, count, body, 0)


def row_of(view, disp, row_count):
    group = lax.axis_size("view") * lax.axis_size("disp")
    return (view * lax.axis_size("disp") + disp) * row_count // group


def match_kernel(
    views, slots, row_count, meta_ref, bands_ref, out_ref,
    pad_ref, roll_ref, stat_ref, tail_ref, patch_ref,
    left_cols, left_rows, right_cols, right_rows, score_ref, result_ref,
):
    cols = patch_ref.shape[1]
    out_ref[...] = jnp.zeros_like(out_ref)
    pad_ref[...] = jnp.zeros_like(pad_ref)
    column = lax.broadcasted_iota(jnp.int32, (1, cols), 1)
    depth_at = lax.broadcasted_iota(jnp.int32, (1, DEPTH), 1) - 27 * TAPS
    ones = jnp.ones((1, cols), jnp.float32)
    flag = jnp.where((depth_at >= 0) & (depth_at < 6), 1.0, 0.0)
    local = row_of(lax.axis_index("view"), lax.axis_index("disp"), row_count)
    row = (lax.axis_index("row") * row_count + local).astype(jnp.float32)
    for view in range(views):
        moved = pltpu.roll(bands_ref[view], 2 * row_count + RAD - local, 0)
        pad_ref[view, 0:TAPS, PAD : PAD + cols] = moved[0:TAPS]
    for view in range(1, views):
        build_patches(
            pad_ref.at[view], stat_ref, tail_ref, patch_ref, 1.0, None,
            [(3, ones), (4, ones), (5, ones)], (0, 1, 0),
        )
        whole = patch_ref[...].astype(jnp.bfloat16)
        right_cols[view - 1] = whole
        right_rows[view - 1, 0:DISP, :] = jnp.broadcast_to(flag, (DISP, DEPTH)).astype(jnp.bfloat16)
        right_rows[view - 1, DISP : DISP + cols, :] = whole.T
    for view in range(views - 1):
        for slot in range(min(slots, views - 1 - view)):
            partner = view + slot + 1
            pairing = meta_ref[view, 0, 1 + slot]
            first_row = meta_ref[view, 0, 1 + 2 * slots + 2 * slot]
            end_row = meta_ref[view, 0, 2 + 2 * slots + 2 * slot]

            @pl.when((pairing != 0.0) & (row >= first_row) & (row < end_row))
            def _():
                shift = meta_ref[view, 0, 1 + slots + slot].astype(jnp.int32)
                keep = jnp.full((1, cols), pairing, jnp.float32)
                gain = meta_ref[view, 0, 0] * math.log2(math.e)
                roll_ref[...] = pltpu.roll(pad_ref[view], cols + 2 * PAD - shift, 1)
                valid = column < cols - shift
                floor = [-part for part in split3(jnp.full((1, cols), gain, jnp.float32))]
                extras = [(place, floor[place]) for place in range(3)]
                extras += [(place + 3, jnp.where(valid, 0.0, floor[place])) for place in range(3)]
                build_patches(
                    roll_ref, stat_ref, tail_ref, patch_ref, gain, valid, extras, (0, 0, 1)
                )
                whole = patch_ref[...].astype(jnp.bfloat16)
                left_cols[...] = whole
                left_rows[0:cols, :] = whole.T
                splits = [-part for part in split3(jnp.full((1, DEPTH), gain, jnp.float32))]
                ends = jnp.zeros((1, DEPTH), jnp.float32)
                for place in range(6):
                    ends = jnp.where(depth_at == place, splits[place % 3], ends)
                left_rows[cols : cols + DISP, :] = jnp.broadcast_to(ends, (DISP, DEPTH)).astype(jnp.bfloat16)
                soft_side(right_rows.at[partner - 1], left_cols, score_ref, result_ref, True)
                moved = pltpu.roll(jnp.broadcast_to(result_ref[...], (8, cols)), shift, 1)[0:1]
                even = (DISP - 1) / (2.0 * DISP)
                out_ref[view, slot : slot + 1, :] = jnp.where(column < shift, even, moved) * keep
                soft_side(left_rows, right_cols.at[partner - 1], score_ref, result_ref, False)
                place = slots + slot
                out_ref[partner, place : place + 1, :] = result_ref[...] * keep


def match(meta, bands, slots):
    views, rows, cols = bands.shape
    smem = pl.BlockSpec(memory_space=pltpu.SMEM)
    vmem = pl.BlockSpec(memory_space=pltpu.VMEM)
    wide = cols + 2 * PAD
    return pl.pallas_call(
        functools.partial(match_kernel, views, slots, rows // 3),
        out_shape=jax.ShapeDtypeStruct((views, 2 * slots, cols), jnp.float32),
        in_specs=[smem, vmem],
        out_specs=vmem,
        scratch_shapes=[
            pltpu.VMEM((views, 16, wide), jnp.float32),
            pltpu.VMEM((16, wide), jnp.float32),
            pltpu.VMEM((8, wide), jnp.float32),
            pltpu.VMEM((16, cols), jnp.float32),
            pltpu.VMEM((DEPTH, cols), jnp.float32),
            pltpu.VMEM((DEPTH, cols), jnp.bfloat16),
            pltpu.VMEM((cols + DISP, DEPTH), jnp.bfloat16),
            pltpu.VMEM((views - 1, DEPTH, cols), jnp.bfloat16),
            pltpu.VMEM((views - 1, cols + DISP, DEPTH), jnp.bfloat16),
            pltpu.VMEM((512, 256), jnp.float32),
            pltpu.VMEM((1, cols), jnp.float32),
        ],
        compiler_params=pltpu.CompilerParams(vmem_limit_bytes=40 * 1024 * 1024),
        name="match",
    )(meta, bands)


def signal(view, row, disp):
    pl.semaphore_signal(
        pltpu.get_barrier_semaphore(),
        inc=1,
        device_id={"view": view, "row": row, "disp": disp},
        device_id_type=pl.DeviceIdType.MESH,
    )


def remote(source, target, send_sem, recv_sem, view, row, disp):
    return pltpu.make_async_remote_copy(
        src_ref=source,
        dst_ref=target,
        send_sem=send_sem,
        recv_sem=recv_sem,
        device_id={"view": view, "row": row, "disp": disp},
        device_id_type=pl.DeviceIdType.MESH,
    )


def gather_kernel(
    image_ref, pack_ref, bands_ref, meta_ref,
    band_send, band_recv, pack_send, pack_recv, low_send, low_recv, high_send, high_recv,
):
    count = image_ref.shape[0]
    views, bands, disps = (lax.axis_size(axis) for axis in ("view", "row", "disp"))
    view, band, disp = (lax.axis_index(axis) for axis in ("view", "row", "disp"))
    wants_low = [row_of(other, 0, count) < RAD for other in range(views)]
    wants_high = [row_of(other, disps - 1, count) + RAD >= count for other in range(views)]
    get_low = (row_of(view, 0, count) < RAD) & (band > 0)
    get_high = (row_of(view, disps - 1, count) + RAD >= count) & (band < bands - 1)
    has_next = band < bands - 1
    has_previous = band > 0

    for other in range(views):

        @pl.when(view != other)
        def _():
            signal(other, band, disp)

        @pl.when(get_low)
        def _():
            signal(other, band - 1, disp)

        @pl.when(get_high)
        def _():
            signal(other, band + 1, disp)

    expected = views - 1
    expected = expected + jnp.where(has_next, sum(wants_low), 0)
    expected = expected + jnp.where(has_previous, sum(wants_high), 0)
    pl.semaphore_wait(pltpu.get_barrier_semaphore(), expected)

    def band_copy(slot, place, other):
        return remote(
            image_ref, bands_ref.at[place, pl.ds(count, count)],
            band_send.at[slot], band_recv.at[place], other, band, disp,
        )

    def pack_copy(slot, place, other):
        return remote(
            pack_ref, meta_ref.at[place],
            pack_send.at[slot], pack_recv.at[place], other, band, disp,
        )

    def low_copy(slot, place, other):
        return remote(
            image_ref.at[pl.ds(count - RAD, RAD)], bands_ref.at[place, pl.ds(count - RAD, RAD)],
            low_send.at[slot], low_recv.at[place], other, band + 1, disp,
        )

    def high_copy(slot, place, other):
        return remote(
            image_ref.at[pl.ds(0, RAD)], bands_ref.at[place, pl.ds(2 * count, RAD)],
            high_send.at[slot], high_recv.at[place], other, band - 1, disp,
        )

    def sending(step):
        for other in range(views):

            @pl.when(view != other)
            def _():
                step(band_copy(other, view, other))
                step(pack_copy(other, view, other))

            if wants_low[other]:

                @pl.when(has_next)
                def _():
                    step(low_copy(other, view, other))

            if wants_high[other]:

                @pl.when(has_previous)
                def _():
                    step(high_copy(other, view, other))

    sending(lambda copy: copy.start())
    bands_ref[view, pl.ds(count, count), :] = image_ref[...]
    meta_ref[view] = pack_ref[...]

    @pl.when(band == 0)
    def _():
        bands_ref[:, 0:count, :] = jnp.zeros((views, count, image_ref.shape[1]), jnp.float32)

    @pl.when(band == bands - 1)
    def _():
        bands_ref[:, 2 * count : 3 * count, :] = jnp.zeros((views, count, image_ref.shape[1]), jnp.float32)

    for other in range(views):

        @pl.when(view != other)
        def _():
            band_copy(other, other, other).wait_recv()
            pack_copy(other, other, other).wait_recv()

        @pl.when(get_low)
        def _():
            low_copy(other, other, other).wait_recv()

        @pl.when(get_high)
        def _():
            high_copy(other, other, other).wait_recv()

    sending(lambda copy: copy.wait_send())


def gather(image, pack):
    views = lax.axis_size("view")
    rows, cols = image.shape
    vmem = pl.BlockSpec(memory_space=pltpu.VMEM)
    return pl.pallas_call(
        gather_kernel,
        out_shape=(
            jax.ShapeDtypeStruct((views, 3 * rows, cols), jnp.float32),
            jax.ShapeDtypeStruct((views,) + pack.shape, jnp.float32),
        ),
        in_specs=[vmem, vmem],
        out_specs=(vmem, vmem),
        scratch_shapes=[pltpu.SemaphoreType.DMA((views,))] * 8,
        compiler_params=pltpu.CompilerParams(collective_id=0, has_side_effects=True),
        name="gather",
    )(image, pack)


def scatter_kernel(row_count, found_ref, left_ref, right_ref, held_ref, send_sem, recv_sem):
    views, disps = (lax.axis_size(axis) for axis in ("view", "disp"))
    view, band, disp = (lax.axis_index(axis) for axis in ("view", "row", "disp"))
    group = views * disps
    share = group // row_count
    member = view * disps + disp
    mine = row_of(view, disp, row_count)
    sends = member % share == 0
    slots = left_ref.shape[0]
    for row in range(row_count):
        source = row * share

        @pl.when(member != source)
        def _():
            signal(source // disps, band, source % disps)

    @pl.when(sends)
    def _():
        pl.semaphore_wait(pltpu.get_barrier_semaphore(), group - 1)

    def copy(slot, row, place):
        return remote(
            found_ref.at[place // disps], held_ref.at[row],
            send_sem.at[slot], recv_sem.at[row], place // disps, band, place % disps,
        )

    def sending(step):
        for other in range(group):

            @pl.when(sends & (member != other))
            def _():
                step(copy(other, mine, other))

    sending(lambda item: item.start())

    @pl.when(sends)
    def _():
        held_ref[mine] = found_ref[view]

    for row in range(row_count):

        @pl.when(member != row * share)
        def _():
            copy(row, row, row * share).wait_recv()

    for slot in range(slots):
        left_ref[slot] = held_ref[:, slot, :]
        right_ref[slot] = held_ref[:, slots + slot, :]
    sending(lambda item: item.wait_send())


def scatter(found, row_count):
    views, rows, cols = found.shape
    vmem = pl.BlockSpec(memory_space=pltpu.VMEM)
    out = jax.ShapeDtypeStruct((rows // 2, row_count, cols), jnp.float32)
    group = views * lax.axis_size("disp")
    return pl.pallas_call(
        functools.partial(scatter_kernel, row_count),
        out_shape=(out, out),
        in_specs=[vmem],
        out_specs=(vmem, vmem),
        scratch_shapes=[
            pltpu.VMEM((row_count, rows, cols), jnp.float32),
            pltpu.SemaphoreType.DMA((group,)),
            pltpu.SemaphoreType.DMA((row_count,)),
        ],
        compiler_params=pltpu.CompilerParams(collective_id=1, has_side_effects=True),
        name="scatter",
    )(found)


def shards(images, sharpness, paired, offset, row_range):
    image = images[0]
    slots = paired.shape[1]
    ints = jnp.concatenate([paired[0], offset[0], row_range[0].reshape(-1)])
    packed = jnp.concatenate([sharpness, ints.astype(jnp.float32)])
    packed = jnp.pad(packed[None], ((0, 7), (0, 128 - packed.shape[0])))
    bands, meta = gather(image, packed)
    found = match(meta, bands, slots)
    left, right = scatter(found, image.shape[0])
    return (left[None], right[None])


def solution(mesh):
    return jax.shard_map(
        shards,
        mesh=mesh,
        in_specs=(
            P("view", "row", None),
            P("view"),
            P("view", None),
            P("view", None),
            P("view", None, None),
        ),
        out_specs=(P("view", None, "row", None), P("view", None, "row", None)),
        check_vma=False,
    )
```

```python
import functools
import math

import jax
import jax.numpy as jnp
from jax import lax
from jax.experimental import pallas as pl
from jax.experimental.pallas import tpu as pltpu
from jax.sharding import PartitionSpec as P

DISP = 256
RAD = 4
TAPS = 2 * RAD + 1
EPSILON = 1e-05
DEPTH = 256
PAD = 128
FAR = -1e30


def rounded(value):
    return value.astype(jnp.bfloat16).astype(jnp.float32)


def split3(value):
    high = rounded(value)
    middle = rounded(value - high)
    return (high, middle, value - high - middle)


def build_patches(pad_ref, stat_ref, tail_ref, patch_ref, gain, valid, extras, order):
    cols = patch_ref.shape[1]
    top = pad_ref[0:8, :]
    last = pad_ref[8:9, :]
    stat_ref[0:1, :] = jnp.sum(top, axis=0, keepdims=True) + last
    stat_ref[1:2, :] = jnp.sum(top * top, axis=0, keepdims=True) + last * last
    total = stat_ref[0:2, PAD - RAD : PAD - RAD + cols]
    for tap in range(1, TAPS):
        begin = PAD - RAD + tap
        total = total + stat_ref[0:2, begin : begin + cols]
    total = total * (1.0 / (TAPS * TAPS))
    mean = total[0:1]
    var = total[1:2] - mean * mean
    scale = lax.rsqrt(var + EPSILON) * (gain * (1.0 / TAPS))
    if valid is not None:
        scale = jnp.where(valid, scale, 0.0)
    for tap in range(TAPS):
        begin = PAD - RAD + tap
        tail_ref[tap : tap + 1, :] = pad_ref[8:9, begin : begin + cols]
        value = (pad_ref[0:8, begin : begin + cols] - mean) * scale
        high = rounded(value)
        parts = (high, value - high)
        for group in range(3):
            start = group * 8 * TAPS + tap * 8
            patch_ref[start : start + 8, :] = parts[order[group]]
    value = (tail_ref[0:TAPS, :] - mean) * scale
    high = rounded(value)
    parts = (high, value - high)
    for group in range(3):
        start = 24 * TAPS + group * TAPS
        patch_ref[start : start + TAPS, :] = parts[order[group]]
    base = 27 * TAPS
    patch_ref[base:DEPTH, :] = jnp.zeros((DEPTH - base, cols), jnp.float32)
    for place, row in extras:
        patch_ref[base + place : base + place + 1, :] = row


def soft_block(score_ref, result_ref, start, left):
    lane = lax.broadcasted_iota(jnp.int32, (8, 128), 1)
    sub = lax.broadcasted_iota(jnp.int32, (8, 128), 0)
    skew = lane - sub
    sub_f = sub.astype(jnp.float32)
    lane_f = lane[0:1].astype(jnp.float32)
    slack = 0 if left else 1
    steps = DISP // 8
    corner = 128 // 8
    for half in range(2):

        def load(step):
            row = half * 128 + step * 8
            return score_ref[row : row + 8, half * 128 : half * 128 + 128]

        near = [skew < 8 * step + slack for step in range(corner)]
        scores = [jnp.where(near[step], load(step), load(step + steps)) for step in range(corner)]
        scores += [load(step) for step in range(corner, steps)]
        tops = scores[:4]
        for step in range(4, steps):
            tops[step % 4] = jnp.maximum(tops[step % 4], scores[step])
        top = jnp.maximum(jnp.maximum(tops[0], tops[1]), jnp.maximum(tops[2], tops[3]))
        top = jnp.broadcast_to(jnp.max(top, axis=0, keepdims=True), (8, 128))
        zero = jnp.zeros((8, 128), jnp.float32)
        summed, running, far = ([zero, zero], [zero, zero], [zero, zero])
        for step in range(steps):
            weight = jnp.exp2(scores[step] - top)
            if step < corner:
                far[step % 2] = far[step % 2] + jnp.where(near[step], 0.0, weight)
            summed[step % 2] = summed[step % 2] + weight
            running[step % 2] = running[step % 2] + summed[step % 2]
        both = summed[0] + summed[1]
        moment = 8.0 * (steps * both - 2.0 * (running[0] + running[1]) + summed[1])
        moment = moment + sub_f * both + float(DISP) * (far[0] + far[1])
        total = jnp.sum(both, axis=0, keepdims=True)
        moment = jnp.sum(moment, axis=0, keepdims=True)
        if left:
            weighted = (lane_f + DISP) * total - moment
        else:
            weighted = moment - lane_f * total
        column = pl.multiple_of(start + half * 128, 128)
        result_ref[:, pl.ds(column, 128)] = weighted / (total * DISP)


def soft_both(left_rows, left_cols, right_rows, right_cols, left_score, right_score, left_result, right_result):
    count = left_result.shape[1] // 256

    def scores(rows_ref, cols_ref, score_ref, start):
        score_ref[...] = jnp.dot(
            rows_ref[pl.ds(start, 512), :],
            cols_ref[:, pl.ds(start, 256)],
            preferred_element_type=jnp.float32,
        )

    unroll = math.gcd(count, 4)

    def body(step, carry):
        for inner in range(unroll):
            block = step * unroll + inner
            start = pl.multiple_of(block * 256, 256)
            after = pl.multiple_of(jnp.minimum(block + 1, count - 1) * 256, 256)
            scores(left_rows, right_cols, right_score, start)
            soft_block(left_score, left_result, start, True)
            scores(right_rows, left_cols, left_score, after)
            soft_block(right_score, right_result, start, False)
        return carry

    scores(right_rows, left_cols, left_score, 0)
    lax.fori_loop(0, count // unroll, body, 0)


def row_of(view, disp, row_count):
    group = lax.axis_size("view") * lax.axis_size("disp")
    return (view * lax.axis_size("disp") + disp) * row_count // group


def match_kernel(
    views, slots, row_count, meta_ref, bands_ref, out_ref,
    pad_ref, roll_ref, stat_ref, tail_ref, patch_ref,
    left_cols, left_rows, right_cols, right_rows, left_score, right_score, left_result, right_result,
):
    cols = patch_ref.shape[1]
    out_ref[...] = jnp.zeros_like(out_ref)
    pad_ref[...] = jnp.zeros_like(pad_ref)
    column = lax.broadcasted_iota(jnp.int32, (1, cols), 1)
    depth_at = lax.broadcasted_iota(jnp.int32, (1, DEPTH), 1) - 27 * TAPS
    ones = jnp.ones((1, cols), jnp.float32)
    flag = jnp.where((depth_at >= 0) & (depth_at < 6), 1.0, 0.0)
    local = row_of(lax.axis_index("view"), lax.axis_index("disp"), row_count)
    row = (lax.axis_index("row") * row_count + local).astype(jnp.float32)
    for view in range(views):
        moved = pltpu.roll(bands_ref[view], 2 * row_count + RAD - local, 0)
        pad_ref[view, 0:TAPS, PAD : PAD + cols] = moved[0:TAPS]
    for view in range(1, views):
        build_patches(
            pad_ref.at[view], stat_ref, tail_ref, patch_ref, 1.0, None,
            [(3, ones), (4, ones), (5, ones)], (0, 1, 0),
        )
        whole = patch_ref[...].astype(jnp.bfloat16)
        right_cols[view - 1] = whole
        right_rows[view - 1, 0:DISP, :] = jnp.broadcast_to(flag, (DISP, DEPTH)).astype(jnp.bfloat16)
        right_rows[view - 1, DISP : DISP + cols, :] = whole.T
    for view in range(views - 1):
        for slot in range(min(slots, views - 1 - view)):
            partner = view + slot + 1
            pairing = meta_ref[view, 0, 1 + slot]
            first_row = meta_ref[view, 0, 1 + 2 * slots + 2 * slot]
            end_row = meta_ref[view, 0, 2 + 2 * slots + 2 * slot]

            @pl.when((pairing != 0.0) & (row >= first_row) & (row < end_row))
            def _():
                shift = meta_ref[view, 0, 1 + slots + slot].astype(jnp.int32)
                keep = jnp.full((1, cols), pairing, jnp.float32)
                gain = meta_ref[view, 0, 0] * math.log2(math.e)
                roll_ref[...] = pltpu.roll(pad_ref[view], cols + 2 * PAD - shift, 1)
                valid = column < cols - shift
                floor = [-part for part in split3(jnp.full((1, cols), gain, jnp.float32))]
                extras = [(place, floor[place]) for place in range(3)]
                extras += [(place + 3, jnp.where(valid, 0.0, floor[place])) for place in range(3)]
                build_patches(
                    roll_ref, stat_ref, tail_ref, patch_ref, gain, valid, extras, (0, 0, 1)
                )
                whole = patch_ref[...].astype(jnp.bfloat16)
                left_cols[...] = whole
                left_rows[0:cols, :] = whole.T
                splits = [-part for part in split3(jnp.full((1, DEPTH), gain, jnp.float32))]
                ends = jnp.zeros((1, DEPTH), jnp.float32)
                for place in range(6):
                    ends = jnp.where(depth_at == place, splits[place % 3], ends)
                left_rows[cols : cols + DISP, :] = jnp.broadcast_to(ends, (DISP, DEPTH)).astype(jnp.bfloat16)
                soft_both(
                    left_rows, left_cols, right_rows.at[partner - 1], right_cols.at[partner - 1],
                    left_score, right_score, left_result, right_result,
                )
                moved = pltpu.roll(jnp.broadcast_to(left_result[...], (8, cols)), shift, 1)[0:1]
                even = (DISP - 1) / (2.0 * DISP)
                out_ref[view, slot : slot + 1, :] = jnp.where(column < shift, even, moved) * keep
                place = slots + slot
                out_ref[partner, place : place + 1, :] = right_result[...] * keep


def match(meta, bands, slots):
    views, rows, cols = bands.shape
    smem = pl.BlockSpec(memory_space=pltpu.SMEM)
    vmem = pl.BlockSpec(memory_space=pltpu.VMEM)
    wide = cols + 2 * PAD
    return pl.pallas_call(
        functools.partial(match_kernel, views, slots, rows // 3),
        out_shape=jax.ShapeDtypeStruct((views, 2 * slots, cols), jnp.float32),
        in_specs=[smem, vmem],
        out_specs=vmem,
        scratch_shapes=[
            pltpu.VMEM((views, 16, wide), jnp.float32),
            pltpu.VMEM((16, wide), jnp.float32),
            pltpu.VMEM((8, wide), jnp.float32),
            pltpu.VMEM((16, cols), jnp.float32),
            pltpu.VMEM((DEPTH, cols), jnp.float32),
            pltpu.VMEM((DEPTH, cols), jnp.bfloat16),
            pltpu.VMEM((cols + DISP, DEPTH), jnp.bfloat16),
            pltpu.VMEM((views - 1, DEPTH, cols), jnp.bfloat16),
            pltpu.VMEM((views - 1, cols + DISP, DEPTH), jnp.bfloat16),
            pltpu.VMEM((512, 256), jnp.float32),
            pltpu.VMEM((512, 256), jnp.float32),
            pltpu.VMEM((1, cols), jnp.float32),
            pltpu.VMEM((1, cols), jnp.float32),
        ],
        compiler_params=pltpu.CompilerParams(vmem_limit_bytes=40 * 1024 * 1024),
        name="match",
    )(meta, bands)


def signal(view, row, disp):
    pl.semaphore_signal(
        pltpu.get_barrier_semaphore(),
        inc=1,
        device_id={"view": view, "row": row, "disp": disp},
        device_id_type=pl.DeviceIdType.MESH,
    )


def remote(source, target, send_sem, recv_sem, view, row, disp):
    return pltpu.make_async_remote_copy(
        src_ref=source,
        dst_ref=target,
        send_sem=send_sem,
        recv_sem=recv_sem,
        device_id={"view": view, "row": row, "disp": disp},
        device_id_type=pl.DeviceIdType.MESH,
    )


def gather_kernel(
    image_ref, pack_ref, bands_ref, meta_ref,
    band_send, band_recv, pack_send, pack_recv, low_send, low_recv, high_send, high_recv,
):
    count = image_ref.shape[0]
    views, bands, disps = (lax.axis_size(axis) for axis in ("view", "row", "disp"))
    view, band, disp = (lax.axis_index(axis) for axis in ("view", "row", "disp"))
    wants_low = [row_of(other, 0, count) < RAD for other in range(views)]
    wants_high = [row_of(other, disps - 1, count) + RAD >= count for other in range(views)]
    get_low = (row_of(view, 0, count) < RAD) & (band > 0)
    get_high = (row_of(view, disps - 1, count) + RAD >= count) & (band < bands - 1)
    has_next = band < bands - 1
    has_previous = band > 0

    for other in range(views):

        @pl.when(view != other)
        def _():
            signal(other, band, disp)

        @pl.when(get_low)
        def _():
            signal(other, band - 1, disp)

        @pl.when(get_high)
        def _():
            signal(other, band + 1, disp)

    expected = views - 1
    expected = expected + jnp.where(has_next, sum(wants_low), 0)
    expected = expected + jnp.where(has_previous, sum(wants_high), 0)
    pl.semaphore_wait(pltpu.get_barrier_semaphore(), expected)

    def band_copy(slot, place, other):
        return remote(
            image_ref, bands_ref.at[place, pl.ds(count, count)],
            band_send.at[slot], band_recv.at[place], other, band, disp,
        )

    def pack_copy(slot, place, other):
        return remote(
            pack_ref, meta_ref.at[place],
            pack_send.at[slot], pack_recv.at[place], other, band, disp,
        )

    def low_copy(slot, place, other):
        return remote(
            image_ref.at[pl.ds(count - RAD, RAD)], bands_ref.at[place, pl.ds(count - RAD, RAD)],
            low_send.at[slot], low_recv.at[place], other, band + 1, disp,
        )

    def high_copy(slot, place, other):
        return remote(
            image_ref.at[pl.ds(0, RAD)], bands_ref.at[place, pl.ds(2 * count, RAD)],
            high_send.at[slot], high_recv.at[place], other, band - 1, disp,
        )

    def sending(step):
        for other in range(views):

            @pl.when(view != other)
            def _():
                step(band_copy(other, view, other))
                step(pack_copy(other, view, other))

            if wants_low[other]:

                @pl.when(has_next)
                def _():
                    step(low_copy(other, view, other))

            if wants_high[other]:

                @pl.when(has_previous)
                def _():
                    step(high_copy(other, view, other))

    sending(lambda copy: copy.start())
    bands_ref[view, pl.ds(count, count), :] = image_ref[...]
    meta_ref[view] = pack_ref[...]

    @pl.when(band == 0)
    def _():
        bands_ref[:, 0:count, :] = jnp.zeros((views, count, image_ref.shape[1]), jnp.float32)

    @pl.when(band == bands - 1)
    def _():
        bands_ref[:, 2 * count : 3 * count, :] = jnp.zeros((views, count, image_ref.shape[1]), jnp.float32)

    for other in range(views):

        @pl.when(view != other)
        def _():
            band_copy(other, other, other).wait_recv()
            pack_copy(other, other, other).wait_recv()

        @pl.when(get_low)
        def _():
            low_copy(other, other, other).wait_recv()

        @pl.when(get_high)
        def _():
            high_copy(other, other, other).wait_recv()

    sending(lambda copy: copy.wait_send())


def gather(image, pack):
    views = lax.axis_size("view")
    rows, cols = image.shape
    vmem = pl.BlockSpec(memory_space=pltpu.VMEM)
    return pl.pallas_call(
        gather_kernel,
        out_shape=(
            jax.ShapeDtypeStruct((views, 3 * rows, cols), jnp.float32),
            jax.ShapeDtypeStruct((views,) + pack.shape, jnp.float32),
        ),
        in_specs=[vmem, vmem],
        out_specs=(vmem, vmem),
        scratch_shapes=[pltpu.SemaphoreType.DMA((views,))] * 8,
        compiler_params=pltpu.CompilerParams(collective_id=0, has_side_effects=True),
        name="gather",
    )(image, pack)


def scatter_kernel(row_count, found_ref, left_ref, right_ref, held_ref, send_sem, recv_sem):
    views, disps = (lax.axis_size(axis) for axis in ("view", "disp"))
    view, band, disp = (lax.axis_index(axis) for axis in ("view", "row", "disp"))
    group = views * disps
    share = group // row_count
    member = view * disps + disp
    mine = row_of(view, disp, row_count)
    sends = member % share == 0
    slots = left_ref.shape[0]
    for row in range(row_count):
        source = row * share

        @pl.when(member != source)
        def _():
            signal(source // disps, band, source % disps)

    @pl.when(sends)
    def _():
        pl.semaphore_wait(pltpu.get_barrier_semaphore(), group - 1)

    def copy(slot, row, place):
        return remote(
            found_ref.at[place // disps], held_ref.at[row],
            send_sem.at[slot], recv_sem.at[row], place // disps, band, place % disps,
        )

    def sending(step):
        for other in range(group):

            @pl.when(sends & (member != other))
            def _():
                step(copy(other, mine, other))

    sending(lambda item: item.start())

    @pl.when(sends)
    def _():
        held_ref[mine] = found_ref[view]

    for row in range(row_count):

        @pl.when(member != row * share)
        def _():
            copy(row, row, row * share).wait_recv()

    for slot in range(slots):
        left_ref[slot] = held_ref[:, slot, :]
        right_ref[slot] = held_ref[:, slots + slot, :]
    sending(lambda item: item.wait_send())


def scatter(found, row_count):
    views, rows, cols = found.shape
    vmem = pl.BlockSpec(memory_space=pltpu.VMEM)
    out = jax.ShapeDtypeStruct((rows // 2, row_count, cols), jnp.float32)
    group = views * lax.axis_size("disp")
    return pl.pallas_call(
        functools.partial(scatter_kernel, row_count),
        out_shape=(out, out),
        in_specs=[vmem],
        out_specs=(vmem, vmem),
        scratch_shapes=[
            pltpu.VMEM((row_count, rows, cols), jnp.float32),
            pltpu.SemaphoreType.DMA((group,)),
            pltpu.SemaphoreType.DMA((row_count,)),
        ],
        compiler_params=pltpu.CompilerParams(collective_id=1, has_side_effects=True),
        name="scatter",
    )(found)


def shards(images, sharpness, paired, offset, row_range):
    image = images[0]
    slots = paired.shape[1]
    ints = jnp.concatenate([paired[0], offset[0], row_range[0].reshape(-1)])
    packed = jnp.concatenate([sharpness, ints.astype(jnp.float32)])
    packed = jnp.pad(packed[None], ((0, 7), (0, 128 - packed.shape[0])))
    bands, meta = gather(image, packed)
    found = match(meta, bands, slots)
    left, right = scatter(found, image.shape[0])
    return (left[None], right[None])


def solution(mesh):
    return jax.shard_map(
        shards,
        mesh=mesh,
        in_specs=(
            P("view", "row", None),
            P("view"),
            P("view", None),
            P("view", None),
            P("view", None, None),
        ),
        out_specs=(P("view", None, "row", None), P("view", None, "row", None)),
        check_vma=False,
    )
```
